32 devices in a mesh: win: 2 (over x), tm: 16 (over z, y, core).
Axes of the slice: x: 2, y: 2, z: 4, core: 2. Of those that a mesh axis runs over, the one named last changes fastest.
Arguments:
- samples: bfloat16 [16384, 512], P(('win', 'tm')), parts along dimension 0, may hold values from -6 to 6
- block_pairs: int32 [10, 2], replicated, may hold values from 0 to 3, as said below
Outputs:
- lag_values: float32 [2560, 128, 384], P(('win', 'tm')), parts along dimension 0
- amplitude: float32 [2048, 512], P(('win', 'tm')), parts along dimension 0
The draws below stay inside these ranges and needn't reach their ends.
There are 2 independent parts, one for each index of `win`. The reference program is written for one: setup_inputs(seed, part) draws one part's arguments, and reference() takes and returns one part's arrays. A program takes and returns all parts, laid end to end along the dimension named above; an argument that names none is the same for every part. Nothing has to cross between parts.
Inputs may be any that keep to these rules, and one draw needn't show every extreme that they name: `block_pairs`: every pair (a, b) of blocks with a <= b <= a + 3 and b < 4 appears exactly once, as a row (a, b); the order of the rows is drawn.
All inputs are finite; a program needn't handle non-finite values.
Results may differ from the reference program's by a relative error of at most 0.0061.
Values may be sent and summed in bfloat16 or wider, within the bound.
A program may use at most 320 MiB of HBM per device.

```python
import math
import jax
import jax.numpy as jnp
from jax import lax

NBIN = 1024
SEG = 2048
BLK = 128
NBLK = 4
NCH = 512
REACH = 3
NPAIR = 10
SMOOTH = 8
LAGS = 384
NSEG = 4
NT = 8192


def draw_block_pairs(key, part):
    key = jax.random.fold_in(key, 11)
    candidate_total = NBLK * (REACH + 1)
    first_block = jnp.arange(candidate_total, dtype=jnp.int32) // (REACH + 1)
    distance = jnp.arange(candidate_total, dtype=jnp.int32) % (REACH + 1)
    second_block = first_block + distance
    invalid = (second_block >= NBLK).astype(jnp.int32)
    order_keys = jax.random.permutation(key, candidate_total).astype(jnp.int32) + invalid * candidate_total
    chosen = jnp.argsort(order_keys, stable=True)[0:NPAIR].astype(jnp.int32)
    return jnp.stack([first_block[chosen], second_block[chosen]], axis=1).astype(jnp.int32)


def steps_of(own_key, shape, pieces, least, top_value):
    factor_of = 1.0
    for position, blocks in pieces:
        heights = jax.random.uniform(jax.random.fold_in(jax.random.fold_in(own_key, 6), position), (blocks,), jnp.float32, least / len(pieces), top_value / len(pieces))
        factor_of = factor_of * jnp.repeat(jnp.exp(heights), shape[position] // blocks).reshape((-1,) + (1,) * (len(shape) - 1 - position))
    return factor_of


def centred(rng, extent, deviation, limit, cuts=(), kind=jnp.bfloat16):
    values = deviation * jax.random.normal(rng, extent, jnp.float32)
    if cuts:
        values = values * steps_of(rng, extent, cuts, -0.22, 0.18)
    return jnp.clip(values, -limit, limit).astype(kind)


def setup_inputs(seed: int = 0, part: int = 0) -> dict:
    streams_of = jax.random.split(jax.random.key(seed), 3)
    own_keys = jax.random.split(jax.random.fold_in(streams_of[2], part), 3)
    samples = centred(own_keys[0], (NT, NCH), 1.0, 6.0, ((0, 16),))
    block_pairs = draw_block_pairs(jax.random.fold_in(streams_of[2], 71), part)
    return dict(samples=samples, block_pairs=block_pairs)


def forward_table(first_time, time_count, seg_length, bin_total):
    sample_times = first_time + jnp.arange(time_count, dtype=jnp.int32)
    bin_index = jnp.arange(bin_total, dtype=jnp.int32)
    phases = (sample_times[:, None] * bin_index[None, :] % seg_length).astype(jnp.float32) * (2.0 * math.pi / seg_length)
    return jnp.concatenate([jnp.cos(phases), -jnp.sin(phases)], axis=1).astype(jnp.bfloat16)

def inverse_table(bin_total, seg_length, lag_total):
    bin_index = jnp.arange(bin_total, dtype=jnp.int32)
    lag_offsets = jnp.arange(lag_total, dtype=jnp.int32) - lag_total // 2
    phases = (bin_index[:, None] * lag_offsets[None, :] % seg_length).astype(jnp.float32) * (2.0 * math.pi / seg_length)
    return jnp.stack([jnp.cos(phases), -jnp.sin(phases)], axis=1).astype(jnp.bfloat16)

def reference(samples, block_pairs):
    forward_rows = forward_table(0, SEG, SEG, NBIN)
    segments = samples.reshape(NSEG, SEG, NCH)

    def segment_spectrum(segment):
        return jnp.dot(forward_rows.T, segment, preferred_element_type=jnp.float32) * (1.0 / math.sqrt(SEG))
    spectra = lax.map(segment_spectrum, segments)
    spectra = spectra.reshape(NSEG, 2, NBIN, NCH).transpose(1, 2, 0, 3)
    magnitude = jnp.sqrt(spectra[0] * spectra[0] + spectra[1] * spectra[1])
    column = lax.optimization_barrier(jnp.sum(magnitude, axis=1))
    padded = jnp.pad(column, ((SMOOTH, SMOOTH), (0, 0)))
    window = padded[0:NBIN]
    for offset_bin in range(1, 2 * SMOOTH + 1):
        window = window + padded[offset_bin:offset_bin + NBIN]
    amplitude = window / float((2 * SMOOTH + 1) * NSEG) + 1e-06
    whitened = (spectra / amplitude[None, :, None, :]).astype(jnp.bfloat16)
    inverse_rows = inverse_table(NBIN, SEG, LAGS).astype(jnp.float32)

    def pair_lags(pair_row):
        left_side = lax.dynamic_slice_in_dim(whitened, (pair_row[0] * BLK).astype(jnp.int32), BLK, 3).astype(jnp.float32)
        right_side = lax.dynamic_slice_in_dim(whitened, (pair_row[1] * BLK).astype(jnp.int32), BLK, 3).astype(jnp.float32)
        real_part = jnp.einsum('fsu,fsv->fuv', left_side[0], right_side[0]) + jnp.einsum('fsu,fsv->fuv', left_side[1], right_side[1])
        imag_part = jnp.einsum('fsu,fsv->fuv', left_side[1], right_side[0]) - jnp.einsum('fsu,fsv->fuv', left_side[0], right_side[1])
        cross_spec = (jnp.stack([real_part, imag_part], axis=2) / float(NSEG)).astype(jnp.bfloat16)
        return jnp.einsum('fucv,fcl->uvl', cross_spec.astype(jnp.float32), inverse_rows) * (1.0 / math.sqrt(NBIN))
    lag_values = lax.map(pair_lags, block_pairs).reshape(NPAIR * BLK, BLK, LAGS)
    return (lag_values, amplitude)
```

```python
import functools
import math

import jax
import jax.numpy as jnp
import numpy as np
from jax import lax
from jax.experimental import pallas as pl
from jax.experimental.pallas import tpu as pltpu
from jax.sharding import PartitionSpec as P

NBIN = 1024
SEG = 2048
GROUP = 4
BLK = 128
SMOOTH = 8
LAGS = 384
HALF = SEG // 2
HBIN = NBIN // 2
KCH = 256
MIB = 1024 * 1024

BIN_ORDER = np.concatenate([np.arange(0, NBIN, 2), np.arange(1, NBIN, 2)])


def forward_constant():
    times = np.arange(HALF)[:, None]
    parts = []
    for bins in (BIN_ORDER[:HBIN], BIN_ORDER[HBIN:]):
        phases = (times * bins[None, :] % SEG) * (2.0 * math.pi / SEG)
        parts.append(np.concatenate([np.cos(phases), -np.sin(phases)], axis=1))
    return np.stack(parts).astype(jnp.bfloat16)


def inverse_constant():
    lag_offsets = np.arange(LAGS) - LAGS // 2
    phases = (BIN_ORDER[:, None] * lag_offsets[None, :] % SEG) * (2.0 * math.pi / SEG)
    return np.stack([np.cos(phases), -np.sin(phases)]).astype(jnp.bfloat16)


def band_constant():
    return (np.abs(BIN_ORDER[:, None] - BIN_ORDER[None, :]) <= SMOOTH).astype(jnp.bfloat16)


def whiten_kernel(seg_count, per_step, x_ref, f_ref, band_ref, w_ref, amp_ref, spec, column, inv_amp):
    step = pl.program_id(1)
    rounds = seg_count // per_step

    @pl.when(step < rounds)
    def _():
        sums, diffs = [], []
        for s in range(per_step):
            first = x_ref[s * SEG : s * SEG + HALF, :].astype(jnp.float32)
            second = x_ref[s * SEG + HALF : (s + 1) * SEG, :].astype(jnp.float32)
            sums.append((first + second).astype(jnp.bfloat16).T)
            diffs.append((first - second).astype(jnp.bfloat16).T)
        total = [None, None]
        for i, folded in enumerate((sums, diffs)):
            rows = jnp.concatenate(folded, axis=0)
            for half in range(2):
                q = HBIN // 2
                cols = slice(half * q, (half + 1) * q)
                scale = 1.0 / math.sqrt(SEG)
                re = jnp.dot(rows, f_ref[i, :, half * q : (half + 1) * q], preferred_element_type=jnp.float32) * scale
                im = (
                    jnp.dot(
                        rows,
                        f_ref[i, :, HBIN + half * q : HBIN + (half + 1) * q],
                        preferred_element_type=jnp.float32,
                    )
                    * scale
                )
                magnitude = jnp.sqrt(re * re + im * im)
                at = i * HBIN + half * q
                col = jnp.zeros((BLK, q), jnp.float32)
                for s in range(per_step):
                    piece = slice(s * BLK, (s + 1) * BLK)
                    spec[step * per_step + s, 0, :, at : at + q] = re[piece]
                    spec[step * per_step + s, 1, :, at : at + q] = im[piece]
                    col = col + magnitude[piece]

                @pl.when(step == 0)
                def _():
                    column[:, at : at + q] = col

                @pl.when(step > 0)
                def _():
                    column[:, at : at + q] += col

    @pl.when(step == rounds)
    def _():
        col = column[...]
        high = col.astype(jnp.bfloat16)
        low = (col - high.astype(jnp.float32)).astype(jnp.bfloat16)
        window = jnp.dot(high, band_ref[...], preferred_element_type=jnp.float32) + jnp.dot(
            low, band_ref[...], preferred_element_type=jnp.float32
        )
        amp = window * (1.0 / float((2 * SMOOTH + 1) * seg_count)) + 1e-06
        amp_ref[...] = amp
        inv_amp[...] = 1.0 / amp

    @pl.when(step >= rounds)
    def _():
        for s in range(per_step):
            for c in range(2):
                w_ref[2 * s + c] = (spec[(step - rounds) * per_step + s, c] * inv_amp[...]).astype(jnp.bfloat16)


def whiten(samples, seg_count):
    per_step = min(seg_count, 4)
    rounds = seg_count // per_step
    channels = samples.shape[1]
    return pl.pallas_call(
        functools.partial(whiten_kernel, seg_count, per_step),
        grid=(channels // BLK, 2 * rounds),
        in_specs=[
            pl.BlockSpec((per_step * SEG, BLK), lambda h, s: (jnp.minimum(s, rounds - 1), h)),
            pl.BlockSpec((2, HALF, NBIN), lambda h, s: (0, 0, 0)),
            pl.BlockSpec((NBIN, NBIN), lambda h, s: (0, 0)),
        ],
        out_specs=[
            pl.BlockSpec((2 * per_step, BLK, NBIN), lambda h, s: (jnp.maximum(s - rounds, 0), h, 0)),
            pl.BlockSpec((BLK, NBIN), lambda h, s: (h, 0)),
        ],
        out_shape=[
            jax.ShapeDtypeStruct((2 * seg_count, channels, NBIN), jnp.bfloat16),
            jax.ShapeDtypeStruct((channels, NBIN), jnp.float32),
        ],
        scratch_shapes=[
            pltpu.VMEM((seg_count, 2, BLK, NBIN), jnp.float32),
            pltpu.VMEM((BLK, NBIN), jnp.float32),
            pltpu.VMEM((BLK, NBIN), jnp.float32),
        ],
        compiler_params=pltpu.CompilerParams(vmem_limit_bytes=60 * MIB),
    )(samples, jnp.asarray(forward_constant()), jnp.asarray(band_constant()))


def cross_terms(u_ref, v_ref, row, segs, base, k0):
    re = im = None
    for s in range(segs):
        at = base + 2 * s
        u0 = u_ref[0, at, pl.ds(row, 1), k0 : k0 + KCH]
        u1 = u_ref[0, at + 1, pl.ds(row, 1), k0 : k0 + KCH]
        u0 = jnp.broadcast_to(u0, (16, KCH)).astype(jnp.bfloat16)[None]
        u1 = jnp.broadcast_to(u1, (16, KCH)).astype(jnp.bfloat16)[None]
        v0 = v_ref[at, :, k0 : k0 + KCH].reshape(BLK // 16, 16, KCH)
        v1 = v_ref[at + 1, :, k0 : k0 + KCH].reshape(BLK // 16, 16, KCH)
        r = u0 * v0 + u1 * v1
        i = u1 * v0 - u0 * v1
        re = r if re is None else re + r
        im = i if im is None else im + i
    return re.reshape(BLK, KCH), im.reshape(BLK, KCH)


def lags_kernel(seg_count, together, unit, blocks_ref, u_ref, v_ref, inv_ref, out_ref):
    scale = 1.0 / (seg_count * math.sqrt(NBIN))

    def body(g, carry):
        acc = jnp.zeros((together * BLK, LAGS), jnp.float32)
        for k0 in range(0, NBIN, KCH):
            res, ims = [], []
            for q in range(together):
                row = g * together + q
                if seg_count <= 4:
                    re, im = cross_terms(u_ref, v_ref, row, seg_count, 0, k0)
                else:

                    def more(j, held):
                        re, im = cross_terms(u_ref, v_ref, row, 4, j * 8, k0)
                        return held[0] + re.astype(jnp.float32), held[1] + im.astype(jnp.float32)

                    zero = jnp.zeros((BLK, KCH), jnp.float32)
                    re, im = lax.fori_loop(0, seg_count // 4, more, (zero, zero))
                    re, im = re.astype(jnp.bfloat16), im.astype(jnp.bfloat16)
                res.append(re)
                ims.append(im)
            acc = acc + jnp.dot(
                jnp.concatenate(res, axis=0), inv_ref[0, k0 : k0 + KCH, :], preferred_element_type=jnp.float32
            )
            acc = acc + jnp.dot(
                jnp.concatenate(ims, axis=0), inv_ref[1, k0 : k0 + KCH, :], preferred_element_type=jnp.float32
            )
        for q in range(together):
            out_ref[g * together + q] = acc[q * BLK : (q + 1) * BLK] * scale
        return carry

    lax.fori_loop(0, unit // together, body, 0)


def lags(whitened, left_rows, right_blocks, seg_count):
    groups, _, unit, _ = left_rows.shape
    together = 2 if unit % 2 == 0 else 1
    return pl.pallas_call(
        functools.partial(lags_kernel, seg_count, together, unit),
        grid_spec=pltpu.PrefetchScalarGridSpec(
            num_scalar_prefetch=1,
            grid=(groups,),
            in_specs=[
                pl.BlockSpec((1, 2 * seg_count, unit, NBIN), lambda g, blocks: (g, 0, 0, 0)),
                pl.BlockSpec((2 * seg_count, BLK, NBIN), lambda g, blocks: (0, blocks[g], 0)),
                pl.BlockSpec((2, NBIN, LAGS), lambda g, blocks: (0, 0, 0)),
            ],
            out_specs=pl.BlockSpec((unit, BLK, LAGS), lambda g, blocks: (g, 0, 0)),
        ),
        out_shape=jax.ShapeDtypeStruct((groups * unit, BLK, LAGS), jnp.float32),
        compiler_params=pltpu.CompilerParams(vmem_limit_bytes=60 * MIB),
    )(right_blocks, left_rows, whitened, jnp.asarray(inverse_constant()))


def per_device(samples, block_pairs):
    devices = lax.axis_size("tm")
    position = lax.axis_index("tm")
    shard_len, channels = samples.shape
    seg_count = devices * shard_len // SEG
    bin_count = NBIN // devices
    rows = block_pairs.shape[0] * BLK // devices
    gathered = lax.all_gather(samples, "tm", axis=0, tiled=True)
    whitened, amp = whiten(gathered, seg_count)

    unit = math.gcd(rows, BLK)
    starts = position * rows + unit * jnp.arange(rows // unit, dtype=jnp.int32)
    pair = starts // BLK
    left_starts = block_pairs[pair, 0] * BLK + starts % BLK
    right_blocks = block_pairs[pair, 1]
    left_rows = jnp.stack(
        [
            lax.dynamic_slice_in_dim(whitened, left_starts[g], unit, axis=1).astype(jnp.float32)
            for g in range(rows // unit)
        ]
    )
    lag_values = lags(whitened, left_rows, right_blocks, seg_count)

    half = bin_count // 2
    even = lax.dynamic_slice_in_dim(amp, position * half, half, axis=1)
    odd = lax.dynamic_slice_in_dim(amp, HBIN + position * half, half, axis=1)
    amplitude = jnp.stack([even.T, odd.T], axis=1).reshape(bin_count, channels)
    return (lag_values, amplitude)


def solution(mesh):
    placed = (P(("win", "tm"), None), P())
    return jax.shard_map(
        per_device,
        mesh=mesh,
        in_specs=placed,
        out_specs=(P(("win", "tm"), None, None), P(("win", "tm"), None)),
        check_vma=False,
    )
```

```python
import functools
import math

import jax
import jax.numpy as jnp
import numpy as np
from jax import lax
from jax.experimental import pallas as pl
from jax.experimental.pallas import tpu as pltpu
from jax.sharding import PartitionSpec as P

NBIN = 1024
SEG = 2048
GROUP = 4
BLK = 128
SMOOTH = 8
LAGS = 384
HALF = SEG // 2
HBIN = NBIN // 2
KCH = 256
MIB = 1024 * 1024

BIN_ORDER = np.concatenate([np.arange(0, NBIN, 2), np.arange(1, NBIN, 2)])


def forward_constant():
    times = np.arange(HALF)[:, None]
    parts = []
    for bins in (BIN_ORDER[:HBIN], BIN_ORDER[HBIN:]):
        phases = (times * bins[None, :] % SEG) * (2.0 * math.pi / SEG)
        parts.append(np.concatenate([np.cos(phases), -np.sin(phases)], axis=1))
    return np.stack(parts).astype(jnp.bfloat16)


def inverse_constant():
    lag_offsets = np.arange(LAGS) - LAGS // 2
    phases = (BIN_ORDER[:, None] * lag_offsets[None, :] % SEG) * (2.0 * math.pi / SEG)
    return np.stack([np.cos(phases), -np.sin(phases)]).astype(jnp.bfloat16)


def band_constant():
    return (np.abs(BIN_ORDER[:, None] - BIN_ORDER[None, :]) <= SMOOTH).astype(jnp.bfloat16)


def gather_kernel(layers, x_ref, out_ref, local_sem, send_sem, recv_sem):
    me = lax.axis_index("tm")
    core = lax.rem(me, 2)
    y = lax.rem(lax.div(me, 2), 2)
    z = lax.div(me, 4)
    length = x_ref.shape[0]
    above, below, across, sibling = me + 4, me - 4, me + 2 - 4 * y, me + 1 - 2 * core
    has_above, has_below = z < layers - 1, z > 0

    def slot_of(layer, row, lane):
        return layer * 4 + row * 2 + lane

    def part(slot):
        return out_ref.at[pl.ds(pl.multiple_of(slot * length, length), length), :]

    def copy(kind, slot, target, src=None):
        return pltpu.make_async_remote_copy(
            src_ref=part(slot) if src is None else src,
            dst_ref=part(slot),
            send_sem=send_sem.at[kind, slot],
            recv_sem=recv_sem.at[slot],
            device_id={"tm": target},
            device_id_type=pl.DeviceIdType.MESH,
        )

    def greet(target):
        pl.semaphore_signal(
            barrier, inc=1, device_id={"tm": target}, device_id_type=pl.DeviceIdType.MESH
        )

    barrier = pltpu.get_barrier_semaphore()
    greet(across)
    greet(sibling)
    pl.when(has_above)(lambda: greet(above))
    pl.when(has_below)(lambda: greet(below))
    pl.semaphore_wait(barrier, 2 + jnp.minimum(z, 1) + jnp.minimum(layers - 1 - z, 1))

    own = pltpu.make_async_copy(x_ref, part(me), local_sem)
    pl.when(has_above)(lambda: copy(0, me, above, x_ref).start())
    pl.when(has_below)(lambda: copy(1, me, below, x_ref).start())
    copy(2, me, across, x_ref).start()
    copy(3, me, sibling, x_ref).start()
    own.start()

    def from_across(layer):
        slot = slot_of(layer, 1 - y, core)
        copy(3, slot, sibling).wait_recv()
        copy(3, slot, sibling).start()

    for d in range(1, layers + 1):
        if d < layers:

            @pl.when(z - d >= 0)
            def _():
                slot = slot_of(z - d, y, core)
                copy(0, slot, sibling).wait_recv()
                pl.when(has_above)(lambda: copy(0, slot, above).start())
                copy(2, slot, across).start()
                copy(3, slot, sibling).start()

            @pl.when(z + d < layers)
            def _():
                slot = slot_of(z + d, y, core)
                copy(1, slot, sibling).wait_recv()
                pl.when(has_below)(lambda: copy(1, slot, below).start())
                copy(2, slot, across).start()
                copy(3, slot, sibling).start()

        pl.when(z - (d - 1) >= 0)(lambda: from_across(z - (d - 1)))
        if d > 1:
            pl.when(z + d - 1 < layers)(lambda: from_across(z + d - 1))

    for layer in range(layers):
        for row in range(2):
            copy(3, slot_of(layer, row, 1 - core), sibling).wait_recv()
    own.wait()
    for layer in range(layers):
        slot = slot_of(layer, y, core)
        pl.when(jnp.logical_and(has_above, layer <= z))(lambda: copy(0, slot, above).wait_send())
        pl.when(jnp.logical_and(has_below, layer >= z))(lambda: copy(1, slot, below).wait_send())
        copy(2, slot, across).wait_send()
        copy(3, slot, sibling).wait_send()
        copy(3, slot_of(layer, 1 - y, core), sibling).wait_send()


def gather(samples, devices):
    if devices != 16:
        return lax.all_gather(samples, "tm", axis=0, tiled=True)
    return pl.pallas_call(
        functools.partial(gather_kernel, devices // 4),
        in_specs=[pl.BlockSpec(memory_space=pl.ANY)],
        out_specs=pl.BlockSpec(memory_space=pl.ANY),
        out_shape=jax.ShapeDtypeStruct((devices * samples.shape[0], samples.shape[1]), samples.dtype),
        scratch_shapes=[
            pltpu.SemaphoreType.DMA,
            pltpu.SemaphoreType.DMA((4, devices)),
            pltpu.SemaphoreType.DMA((devices,)),
        ],
        compiler_params=pltpu.CompilerParams(collective_id=0, has_side_effects=True),
    )(samples)


def whiten_kernel(seg_count, per_step, x_ref, f_ref, band_ref, w_ref, amp_ref, spec, column, inv_amp):
    step = pl.program_id(1)
    rounds = seg_count // per_step

    @pl.when(step < rounds)
    def _():
        sums, diffs = [], []
        for s in range(per_step):
            first = x_ref[s * SEG : s * SEG + HALF, :].astype(jnp.float32)
            second = x_ref[s * SEG + HALF : (s + 1) * SEG, :].astype(jnp.float32)
            sums.append((first + second).astype(jnp.bfloat16).T)
            diffs.append((first - second).astype(jnp.bfloat16).T)
        total = [None, None]
        for i, folded in enumerate((sums, diffs)):
            rows = jnp.concatenate(folded, axis=0)
            for half in range(2):
                q = HBIN // 2
                cols = slice(half * q, (half + 1) * q)
                scale = 1.0 / math.sqrt(SEG)
                re = jnp.dot(rows, f_ref[i, :, half * q : (half + 1) * q], preferred_element_type=jnp.float32) * scale
                im = (
                    jnp.dot(
                        rows,
                        f_ref[i, :, HBIN + half * q : HBIN + (half + 1) * q],
                        preferred_element_type=jnp.float32,
                    )
                    * scale
                )
                magnitude = jnp.sqrt(re * re + im * im)
                at = i * HBIN + half * q
                col = jnp.zeros((BLK, q), jnp.float32)
                for s in range(per_step):
                    piece = slice(s * BLK, (s + 1) * BLK)
                    spec[step * per_step + s, 0, :, at : at + q] = re[piece]
                    spec[step * per_step + s, 1, :, at : at + q] = im[piece]
                    col = col + magnitude[piece]

                @pl.when(step == 0)
                def _():
                    column[:, at : at + q] = col

                @pl.when(step > 0)
                def _():
                    column[:, at : at + q] += col

    @pl.when(step == rounds)
    def _():
        col = column[...]
        high = col.astype(jnp.bfloat16)
        low = (col - high.astype(jnp.float32)).astype(jnp.bfloat16)
        window = jnp.dot(high, band_ref[...], preferred_element_type=jnp.float32) + jnp.dot(
            low, band_ref[...], preferred_element_type=jnp.float32
        )
        amp = window * (1.0 / float((2 * SMOOTH + 1) * seg_count)) + 1e-06
        amp_ref[...] = amp
        inv_amp[...] = 1.0 / amp

    @pl.when(step >= rounds)
    def _():
        for s in range(per_step):
            for c in range(2):
                w_ref[2 * s + c] = (spec[(step - rounds) * per_step + s, c] * inv_amp[...]).astype(jnp.bfloat16)


def whiten(samples, seg_count):
    per_step = min(seg_count, 4)
    rounds = seg_count // per_step
    channels = samples.shape[1]
    return pl.pallas_call(
        functools.partial(whiten_kernel, seg_count, per_step),
        grid=(channels // BLK, 2 * rounds),
        in_specs=[
            pl.BlockSpec((per_step * SEG, BLK), lambda h, s: (jnp.minimum(s, rounds - 1), h)),
            pl.BlockSpec((2, HALF, NBIN), lambda h, s: (0, 0, 0)),
            pl.BlockSpec((NBIN, NBIN), lambda h, s: (0, 0)),
        ],
        out_specs=[
            pl.BlockSpec((2 * per_step, BLK, NBIN), lambda h, s: (jnp.maximum(s - rounds, 0), h, 0)),
            pl.BlockSpec((BLK, NBIN), lambda h, s: (h, 0)),
        ],
        out_shape=[
            jax.ShapeDtypeStruct((2 * seg_count, channels, NBIN), jnp.bfloat16),
            jax.ShapeDtypeStruct((channels, NBIN), jnp.float32),
        ],
        scratch_shapes=[
            pltpu.VMEM((seg_count, 2, BLK, NBIN), jnp.float32),
            pltpu.VMEM((BLK, NBIN), jnp.float32),
            pltpu.VMEM((BLK, NBIN), jnp.float32),
        ],
        compiler_params=pltpu.CompilerParams(vmem_limit_bytes=60 * MIB),
    )(samples, jnp.asarray(forward_constant()), jnp.asarray(band_constant()))


def cross_terms(u_ref, v_ref, row, segs, base, k0):
    re = im = None
    for s in range(segs):
        at = base + 2 * s
        u0 = u_ref[at, pl.ds(row, 1), k0 : k0 + KCH]
        u1 = u_ref[at + 1, pl.ds(row, 1), k0 : k0 + KCH]
        u0 = jnp.broadcast_to(u0, (16, KCH)).astype(jnp.bfloat16)[None]
        u1 = jnp.broadcast_to(u1, (16, KCH)).astype(jnp.bfloat16)[None]
        v0 = v_ref[at, :, k0 : k0 + KCH].reshape(BLK // 16, 16, KCH)
        v1 = v_ref[at + 1, :, k0 : k0 + KCH].reshape(BLK // 16, 16, KCH)
        r = u0 * v0 + u1 * v1
        i = u1 * v0 - u0 * v1
        re = r if re is None else re + r
        im = i if im is None else im + i
    return re.reshape(BLK, KCH), im.reshape(BLK, KCH)


def lags_kernel(seg_count, together, unit, lefts_ref, blocks_ref, left_ref, v_ref, inv_ref, out_ref, u_ref):
    scale = 1.0 / (seg_count * math.sqrt(NBIN))
    u_ref[...] = left_ref[...].astype(jnp.float32)

    def body(g, carry):
        acc = jnp.zeros((together * BLK, LAGS), jnp.float32)
        for k0 in range(0, NBIN, KCH):
            res, ims = [], []
            for q in range(together):
                row = g * together + q
                if seg_count <= 4:
                    re, im = cross_terms(u_ref, v_ref, row, seg_count, 0, k0)
                else:

                    def more(j, held):
                        re, im = cross_terms(u_ref, v_ref, row, 4, j * 8, k0)
                        return held[0] + re.astype(jnp.float32), held[1] + im.astype(jnp.float32)

                    zero = jnp.zeros((BLK, KCH), jnp.float32)
                    re, im = lax.fori_loop(0, seg_count // 4, more, (zero, zero))
                    re, im = re.astype(jnp.bfloat16), im.astype(jnp.bfloat16)
                res.append(re)
                ims.append(im)
            acc = acc + jnp.dot(
                jnp.concatenate(res, axis=0), inv_ref[0, k0 : k0 + KCH, :], preferred_element_type=jnp.float32
            )
            acc = acc + jnp.dot(
                jnp.concatenate(ims, axis=0), inv_ref[1, k0 : k0 + KCH, :], preferred_element_type=jnp.float32
            )
        for q in range(together):
            out_ref[g * together + q] = acc[q * BLK : (q + 1) * BLK] * scale
        return carry

    lax.fori_loop(0, unit // together, body, 0)


def lags(whitened, left_rows, left_units, right_blocks, seg_count, unit):
    groups = right_blocks.shape[0]
    together = 2 if unit % 2 == 0 else 1
    if left_rows is None:
        left_rows = whitened
        left_spec = pl.BlockSpec((2 * seg_count, unit, NBIN), lambda g, lefts, blocks: (0, lefts[g], 0))
    else:
        left_spec = pl.BlockSpec((None, 2 * seg_count, unit, NBIN), lambda g, lefts, blocks: (g, 0, 0, 0))
    return pl.pallas_call(
        functools.partial(lags_kernel, seg_count, together, unit),
        grid_spec=pltpu.PrefetchScalarGridSpec(
            num_scalar_prefetch=2,
            grid=(groups,),
            in_specs=[
                left_spec,
                pl.BlockSpec((2 * seg_count, BLK, NBIN), lambda g, lefts, blocks: (0, blocks[g], 0)),
                pl.BlockSpec((2, NBIN, LAGS), lambda g, lefts, blocks: (0, 0, 0)),
            ],
            out_specs=pl.BlockSpec((unit, BLK, LAGS), lambda g, lefts, blocks: (g, 0, 0)),
            scratch_shapes=[pltpu.VMEM((2 * seg_count, unit, NBIN), jnp.float32)],
        ),
        out_shape=jax.ShapeDtypeStruct((groups * unit, BLK, LAGS), jnp.float32),
        compiler_params=pltpu.CompilerParams(vmem_limit_bytes=60 * MIB),
    )(left_units, right_blocks, left_rows, whitened, jnp.asarray(inverse_constant()))


def per_device(samples, block_pairs):
    devices = lax.axis_size("tm")
    position = lax.axis_index("tm")
    shard_len, channels = samples.shape
    seg_count = devices * shard_len // SEG
    bin_count = NBIN // devices
    rows = block_pairs.shape[0] * BLK // devices
    gathered = gather(samples, devices)
    whitened, amp = whiten(gathered, seg_count)

    unit = math.gcd(rows, BLK)
    starts = position * rows + unit * jnp.arange(rows // unit, dtype=jnp.int32)
    pair = starts // BLK
    left_starts = block_pairs[pair, 0] * BLK + starts % BLK
    right_blocks = block_pairs[pair, 1]
    left_rows = None
    if unit % 16:
        left_rows = jnp.stack(
            [
                lax.dynamic_slice_in_dim(whitened, left_starts[g], unit, axis=1)
                for g in range(rows // unit)
            ]
        )
    lag_values = lags(whitened, left_rows, left_starts // unit, right_blocks, seg_count, unit)

    half = bin_count // 2
    even = lax.dynamic_slice_in_dim(amp, position * half, half, axis=1)
    odd = lax.dynamic_slice_in_dim(amp, HBIN + position * half, half, axis=1)
    amplitude = jnp.stack([even.T, odd.T], axis=1).reshape(bin_count, channels)
    return (lag_values, amplitude)


def solution(mesh):
    placed = (P(("win", "tm"), None), P())
    return jax.shard_map(
        per_device,
        mesh=mesh,
        in_specs=placed,
        out_specs=(P(("win", "tm"), None, None), P(("win", "tm"), None)),
        check_vma=False,
    )
```

```python
import functools
import math

import jax
import jax.numpy as jnp
import numpy as np
from jax import lax
from jax.experimental import pallas as pl
from jax.experimental.pallas import tpu as pltpu
from jax.sharding import PartitionSpec as P

NBIN = 1024
SEG = 2048
GROUP = 4
BLK = 128
SMOOTH = 8
LAGS = 384
HALF = SEG // 2
HBIN = NBIN // 2
KCH = 256
PIECES = 2
CHANS = 256
MIB = 1024 * 1024

BIN_ORDER = np.concatenate([np.arange(0, NBIN, 2), np.arange(1, NBIN, 2)])


def forward_constant():
    times = np.arange(HALF)[:, None]
    parts = []
    for bins in (BIN_ORDER[:HBIN], BIN_ORDER[HBIN:]):
        phases = (times * bins[None, :] % SEG) * (2.0 * math.pi / SEG)
        parts.append(np.concatenate([np.cos(phases), -np.sin(phases)], axis=1))
    return np.stack(parts).astype(jnp.bfloat16)


def inverse_constant():
    lag_offsets = np.arange(LAGS) - LAGS // 2
    phases = (BIN_ORDER[:, None] * lag_offsets[None, :] % SEG) * (2.0 * math.pi / SEG)
    return np.stack([np.cos(phases), -np.sin(phases)]).astype(jnp.bfloat16)


def band_constant():
    return (np.abs(BIN_ORDER[:, None] - BIN_ORDER[None, :]) <= SMOOTH).astype(jnp.bfloat16)


def gather_kernel(layers, x_ref, out_ref, local_sem, send_sem, recv_sem):
    me = lax.axis_index("tm")
    core = lax.rem(me, 2)
    y = lax.rem(lax.div(me, 2), 2)
    z = lax.div(me, 4)
    length = x_ref.shape[0]
    height = length // PIECES
    above, below, across, sibling = me + 4, me - 4, me + 2 - 4 * y, me + 1 - 2 * core
    has_above, has_below = z < layers - 1, z > 0

    def slot_of(layer, row, lane):
        return layer * 4 + row * 2 + lane

    def part(slot, piece):
        return out_ref.at[pl.ds(pl.multiple_of(slot * length + piece * height, height), height), :]

    def copy(kind, slot, piece, target, own=False):
        return pltpu.make_async_remote_copy(
            src_ref=x_ref.at[pl.ds(piece * height, height), :] if own else part(slot, piece),
            dst_ref=part(slot, piece),
            send_sem=send_sem.at[kind, slot, piece],
            recv_sem=recv_sem.at[slot, piece],
            device_id={"tm": target},
            device_id_type=pl.DeviceIdType.MESH,
        )

    def greet(target):
        pl.semaphore_signal(
            barrier, inc=1, device_id={"tm": target}, device_id_type=pl.DeviceIdType.MESH
        )

    barrier = pltpu.get_barrier_semaphore()
    greet(across)
    greet(sibling)
    pl.when(has_above)(lambda: greet(above))
    pl.when(has_below)(lambda: greet(below))
    pl.semaphore_wait(barrier, 2 + jnp.minimum(z, 1) + jnp.minimum(layers - 1 - z, 1))

    for piece in range(PIECES):
        pl.when(has_above)(lambda: copy(0, me, piece, above, True).start())
        pl.when(has_below)(lambda: copy(1, me, piece, below, True).start())
        copy(2, me, piece, across, True).start()
        copy(3, me, piece, sibling, True).start()
    own = pltpu.make_async_copy(x_ref, out_ref.at[pl.ds(pl.multiple_of(me * length, length), length), :], local_sem)
    own.start()

    def from_across(layer, piece):
        slot = slot_of(layer, 1 - y, core)
        copy(3, slot, piece, sibling).wait_recv()
        copy(3, slot, piece, sibling).start()

    for d in range(1, layers + 1):
        for piece in range(PIECES):
            if d < layers:

                @pl.when(z - d >= 0)
                def _():
                    slot = slot_of(z - d, y, core)
                    copy(0, slot, piece, sibling).wait_recv()
                    pl.when(has_above)(lambda: copy(0, slot, piece, above).start())
                    copy(2, slot, piece, across).start()
                    copy(3, slot, piece, sibling).start()

                @pl.when(z + d < layers)
                def _():
                    slot = slot_of(z + d, y, core)
                    copy(1, slot, piece, sibling).wait_recv()
                    pl.when(has_below)(lambda: copy(1, slot, piece, below).start())
                    copy(2, slot, piece, across).start()
                    copy(3, slot, piece, sibling).start()

            pl.when(z - (d - 1) >= 0)(lambda: from_across(z - (d - 1), piece))
            if d > 1:
                pl.when(z + d - 1 < layers)(lambda: from_across(z + d - 1, piece))

    for layer in range(layers):
        for row in range(2):
            for piece in range(PIECES):
                copy(3, slot_of(layer, row, 1 - core), piece, sibling).wait_recv()
    own.wait()
    for layer in range(layers):
        slot = slot_of(layer, y, core)
        for piece in range(PIECES):
            pl.when(jnp.logical_and(has_above, layer <= z))(lambda: copy(0, slot, piece, above).wait_send())
            pl.when(jnp.logical_and(has_below, layer >= z))(lambda: copy(1, slot, piece, below).wait_send())
            copy(2, slot, piece, across).wait_send()
            copy(3, slot, piece, sibling).wait_send()
            copy(3, slot_of(layer, 1 - y, core), piece, sibling).wait_send()


def gather(samples, devices):
    if devices != 16:
        return lax.all_gather(samples, "tm", axis=0, tiled=True)
    return pl.pallas_call(
        functools.partial(gather_kernel, devices // 4),
        in_specs=[pl.BlockSpec(memory_space=pl.ANY)],
        out_specs=pl.BlockSpec(memory_space=pl.ANY),
        out_shape=jax.ShapeDtypeStruct((devices * samples.shape[0], samples.shape[1]), samples.dtype),
        scratch_shapes=[
            pltpu.SemaphoreType.DMA,
            pltpu.SemaphoreType.DMA((4, devices, PIECES)),
            pltpu.SemaphoreType.DMA((devices, PIECES)),
        ],
        compiler_params=pltpu.CompilerParams(collective_id=0, has_side_effects=True),
    )(samples)


def whiten_kernel(seg_count, per_step, x_ref, f_ref, band_ref, w_ref, amp_ref, spec, column, inv_amp):
    step = pl.program_id(1)
    rounds = seg_count // per_step
    chans = x_ref.shape[1]

    @pl.when(step < rounds)
    def _():
        sums, diffs = [], []
        for s in range(per_step):
            first = x_ref[s * SEG : s * SEG + HALF, :].astype(jnp.float32)
            second = x_ref[s * SEG + HALF : (s + 1) * SEG, :].astype(jnp.float32)
            sums.append((first + second).astype(jnp.bfloat16).T)
            diffs.append((first - second).astype(jnp.bfloat16).T)
        total = [None, None]
        for i, folded in enumerate((sums, diffs)):
            rows = jnp.concatenate(folded, axis=0)
            for half in range(2):
                q = HBIN // 2
                cols = slice(half * q, (half + 1) * q)
                scale = 1.0 / math.sqrt(SEG)
                re = jnp.dot(rows, f_ref[i, :, half * q : (half + 1) * q], preferred_element_type=jnp.float32) * scale
                im = (
                    jnp.dot(
                        rows,
                        f_ref[i, :, HBIN + half * q : HBIN + (half + 1) * q],
                        preferred_element_type=jnp.float32,
                    )
                    * scale
                )
                magnitude = jnp.sqrt(re * re + im * im)
                at = i * HBIN + half * q
                col = jnp.zeros((chans, q), jnp.float32)
                for s in range(per_step):
                    piece = slice(s * chans, (s + 1) * chans)
                    spec[step * per_step + s, 0, :, at : at + q] = re[piece]
                    spec[step * per_step + s, 1, :, at : at + q] = im[piece]
                    col = col + magnitude[piece]

                @pl.when(step == 0)
                def _():
                    column[:, at : at + q] = col

                @pl.when(step > 0)
                def _():
                    column[:, at : at + q] += col

    @pl.when(step == rounds)
    def _():
        col = column[...]
        high = col.astype(jnp.bfloat16)
        low = (col - high.astype(jnp.float32)).astype(jnp.bfloat16)
        both = jnp.dot(
            jnp.concatenate([high, low], axis=0), band_ref[...], preferred_element_type=jnp.float32
        )
        window = both[:chans] + both[chans:]
        amp = window * (1.0 / float((2 * SMOOTH + 1) * seg_count)) + 1e-06
        amp_ref[...] = amp
        inv_amp[...] = 1.0 / amp

    @pl.when(step >= rounds)
    def _():
        for s in range(per_step):
            for c in range(2):
                w_ref[2 * s + c] = (spec[(step - rounds) * per_step + s, c] * inv_amp[...]).astype(jnp.bfloat16)


def whiten(samples, seg_count):
    per_step = min(seg_count, 4)
    rounds = seg_count // per_step
    channels = samples.shape[1]
    chans = CHANS if rounds == 1 else BLK
    return pl.pallas_call(
        functools.partial(whiten_kernel, seg_count, per_step),
        grid=(channels // chans, 2 * rounds),
        in_specs=[
            pl.BlockSpec((per_step * SEG, chans), lambda h, s: (jnp.minimum(s, rounds - 1), h)),
            pl.BlockSpec((2, HALF, NBIN), lambda h, s: (0, 0, 0)),
            pl.BlockSpec((NBIN, NBIN), lambda h, s: (0, 0)),
        ],
        out_specs=[
            pl.BlockSpec((2 * per_step, chans, NBIN), lambda h, s: (jnp.maximum(s - rounds, 0), h, 0)),
            pl.BlockSpec((chans, NBIN), lambda h, s: (h, 0)),
        ],
        out_shape=[
            jax.ShapeDtypeStruct((2 * seg_count, channels, NBIN), jnp.bfloat16),
            jax.ShapeDtypeStruct((channels, NBIN), jnp.float32),
        ],
        scratch_shapes=[
            pltpu.VMEM((seg_count, 2, chans, NBIN), jnp.float32),
            pltpu.VMEM((chans, NBIN), jnp.float32),
            pltpu.VMEM((chans, NBIN), jnp.float32),
        ],
        compiler_params=pltpu.CompilerParams(vmem_limit_bytes=60 * MIB),
    )(samples, jnp.asarray(forward_constant()), jnp.asarray(band_constant()))


def cross_terms(u_ref, v_ref, row, segs, base, k0):
    re = im = None
    for s in range(segs):
        at = base + 2 * s
        u0 = u_ref[at, pl.ds(row, 1), k0 : k0 + KCH]
        u1 = u_ref[at + 1, pl.ds(row, 1), k0 : k0 + KCH]
        u0 = jnp.broadcast_to(u0, (16, KCH)).astype(jnp.bfloat16)[None]
        u1 = jnp.broadcast_to(u1, (16, KCH)).astype(jnp.bfloat16)[None]
        v0 = v_ref[at, :, k0 : k0 + KCH].reshape(BLK // 16, 16, KCH)
        v1 = v_ref[at + 1, :, k0 : k0 + KCH].reshape(BLK // 16, 16, KCH)
        r = u0 * v0 + u1 * v1
        i = u1 * v0 - u0 * v1
        re = r if re is None else re + r
        im = i if im is None else im + i
    return re.reshape(BLK, KCH), im.reshape(BLK, KCH)


def lags_kernel(seg_count, together, unit, lefts_ref, blocks_ref, left_ref, v_ref, inv_ref, out_ref, u_ref):
    scale = 1.0 / (seg_count * math.sqrt(NBIN))
    u_ref[...] = left_ref[...].astype(jnp.float32)

    def body(g, carry):
        acc = jnp.zeros((together * BLK, LAGS), jnp.float32)
        for k0 in range(0, NBIN, KCH):
            res, ims = [], []
            for q in range(together):
                row = g * together + q
                if seg_count <= 4:
                    re, im = cross_terms(u_ref, v_ref, row, seg_count, 0, k0)
                else:

                    def more(j, held):
                        re, im = cross_terms(u_ref, v_ref, row, 4, j * 8, k0)
                        return held[0] + re.astype(jnp.float32), held[1] + im.astype(jnp.float32)

                    zero = jnp.zeros((BLK, KCH), jnp.float32)
                    re, im = lax.fori_loop(0, seg_count // 4, more, (zero, zero))
                    re, im = re.astype(jnp.bfloat16), im.astype(jnp.bfloat16)
                res.append(re)
                ims.append(im)
            acc = acc + jnp.dot(
                jnp.concatenate(res, axis=0), inv_ref[0, k0 : k0 + KCH, :], preferred_element_type=jnp.float32
            )
            acc = acc + jnp.dot(
                jnp.concatenate(ims, axis=0), inv_ref[1, k0 : k0 + KCH, :], preferred_element_type=jnp.float32
            )
        for q in range(together):
            out_ref[g * together + q] = acc[q * BLK : (q + 1) * BLK] * scale
        return carry

    if unit == together:
        body(0, 0)
    else:
        lax.fori_loop(0, unit // together, body, 0)


def lags(whitened, left_rows, left_units, right_blocks, seg_count, unit):
    groups = right_blocks.shape[0]
    together = math.gcd(unit, 8)
    if left_rows is None:
        left_rows = whitened
        left_spec = pl.BlockSpec((2 * seg_count, unit, NBIN), lambda g, lefts, blocks: (0, lefts[g], 0))
    else:
        left_spec = pl.BlockSpec((None, 2 * seg_count, unit, NBIN), lambda g, lefts, blocks: (g, 0, 0, 0))
    return pl.pallas_call(
        functools.partial(lags_kernel, seg_count, together, unit),
        grid_spec=pltpu.PrefetchScalarGridSpec(
            num_scalar_prefetch=2,
            grid=(groups,),
            in_specs=[
                left_spec,
                pl.BlockSpec((2 * seg_count, BLK, NBIN), lambda g, lefts, blocks: (0, blocks[g], 0)),
                pl.BlockSpec((2, NBIN, LAGS), lambda g, lefts, blocks: (0, 0, 0)),
            ],
            out_specs=pl.BlockSpec((unit, BLK, LAGS), lambda g, lefts, blocks: (g, 0, 0)),
            scratch_shapes=[pltpu.VMEM((2 * seg_count, unit, NBIN), jnp.float32)],
        ),
        out_shape=jax.ShapeDtypeStruct((groups * unit, BLK, LAGS), jnp.float32),
        compiler_params=pltpu.CompilerParams(vmem_limit_bytes=60 * MIB),
    )(left_units, right_blocks, left_rows, whitened, jnp.asarray(inverse_constant()))


def per_device(samples, block_pairs):
    devices = lax.axis_size("tm")
    position = lax.axis_index("tm")
    shard_len, channels = samples.shape
    seg_count = devices * shard_len // SEG
    bin_count = NBIN // devices
    rows = block_pairs.shape[0] * BLK // devices
    gathered = gather(samples, devices)
    whitened, amp = whiten(gathered, seg_count)

    unit = math.gcd(rows, BLK)
    starts = position * rows + unit * jnp.arange(rows // unit, dtype=jnp.int32)
    pair = starts // BLK
    left_starts = block_pairs[pair, 0] * BLK + starts % BLK
    right_blocks = block_pairs[pair, 1]
    left_rows = None
    if unit % 16:
        left_rows = jnp.stack(
            [
                lax.dynamic_slice_in_dim(whitened, left_starts[g], unit, axis=1)
                for g in range(rows // unit)
            ]
        )
    lag_values = lags(whitened, left_rows, left_starts // unit, right_blocks, seg_count, unit)

    half = bin_count // 2
    even = lax.dynamic_slice_in_dim(amp, position * half, half, axis=1)
    odd = lax.dynamic_slice_in_dim(amp, HBIN + position * half, half, axis=1)
    amplitude = jnp.stack([even.T, odd.T], axis=1).reshape(bin_count, channels)
    return (lag_values, amplitude)


def solution(mesh):
    placed = (P(("win", "tm"), None), P())
    return jax.shard_map(
        per_device,
        mesh=mesh,
        in_specs=placed,
        out_specs=(P(("win", "tm"), None, None), P(("win", "tm"), None)),
        check_vma=False,
    )
```

```python
import functools
import math

import jax
import jax.numpy as jnp
import numpy as np
from jax import lax
from jax.experimental import pallas as pl
from jax.experimental.pallas import tpu as pltpu
from jax.sharding import PartitionSpec as P

NBIN = 1024
SEG = 2048
GROUP = 4
BLK = 128
SMOOTH = 8
LAGS = 384
HBIN = NBIN // 2
KCH = 256
PIECES = 2
CHANS = 256
MIB = 1024 * 1024


def forward_constant():
    phases = (np.arange(SEG)[:, None] * np.arange(NBIN)[None, :] % SEG) * (2.0 * math.pi / SEG)
    return np.concatenate([np.cos(phases), -np.sin(phases)], axis=1).astype(jnp.bfloat16)


def inverse_constant():
    lag_offsets = np.arange(LAGS) - LAGS // 2
    phases = (np.arange(NBIN)[:, None] * lag_offsets[None, :] % SEG) * (2.0 * math.pi / SEG)
    return np.stack([np.cos(phases), -np.sin(phases)]).astype(jnp.bfloat16)


def band_constant():
    return (np.abs(np.arange(NBIN)[:, None] - np.arange(NBIN)[None, :]) <= SMOOTH).astype(jnp.bfloat16)


def gather_kernel(layers, x_ref, out_ref, local_sem, send_sem, recv_sem):
    me = lax.axis_index("tm")
    core = lax.rem(me, 2)
    y = lax.rem(lax.div(me, 2), 2)
    z = lax.div(me, 4)
    length = x_ref.shape[0]
    height = length // PIECES
    above, below, across, sibling = me + 4, me - 4, me + 2 - 4 * y, me + 1 - 2 * core
    has_above, has_below = z < layers - 1, z > 0

    def slot_of(layer, row, lane):
        return layer * 4 + row * 2 + lane

    def part(slot, piece):
        return out_ref.at[pl.ds(pl.multiple_of(slot * length + piece * height, height), height), :]

    def copy(kind, slot, piece, target, own=False):
        return pltpu.make_async_remote_copy(
            src_ref=x_ref.at[pl.ds(piece * height, height), :] if own else part(slot, piece),
            dst_ref=part(slot, piece),
            send_sem=send_sem.at[kind, slot, piece],
            recv_sem=recv_sem.at[slot, piece],
            device_id={"tm": target},
            device_id_type=pl.DeviceIdType.MESH,
        )

    def greet(target):
        pl.semaphore_signal(
            barrier, inc=1, device_id={"tm": target}, device_id_type=pl.DeviceIdType.MESH
        )

    barrier = pltpu.get_barrier_semaphore()
    greet(across)
    greet(sibling)
    pl.when(has_above)(lambda: greet(above))
    pl.when(has_below)(lambda: greet(below))
    pl.semaphore_wait(barrier, 2 + jnp.minimum(z, 1) + jnp.minimum(layers - 1 - z, 1))

    for piece in range(PIECES):
        pl.when(has_above)(lambda: copy(0, me, piece, above, True).start())
        pl.when(has_below)(lambda: copy(1, me, piece, below, True).start())
        copy(2, me, piece, across, True).start()
        copy(3, me, piece, sibling, True).start()
    own = pltpu.make_async_copy(x_ref, out_ref.at[pl.ds(pl.multiple_of(me * length, length), length), :], local_sem)
    own.start()

    def from_across(layer, piece):
        slot = slot_of(layer, 1 - y, core)
        copy(3, slot, piece, sibling).wait_recv()
        copy(3, slot, piece, sibling).start()

    for d in range(1, layers + 1):
        for piece in range(PIECES):
            if d < layers:

                @pl.when(z - d >= 0)
                def _():
                    slot = slot_of(z - d, y, core)
                    copy(0, slot, piece, sibling).wait_recv()
                    pl.when(has_above)(lambda: copy(0, slot, piece, above).start())
                    copy(2, slot, piece, across).start()
                    copy(3, slot, piece, sibling).start()

                @pl.when(z + d < layers)
                def _():
                    slot = slot_of(z + d, y, core)
                    copy(1, slot, piece, sibling).wait_recv()
                    pl.when(has_below)(lambda: copy(1, slot, piece, below).start())
                    copy(2, slot, piece, across).start()
                    copy(3, slot, piece, sibling).start()

            pl.when(z - (d - 1) >= 0)(lambda: from_across(z - (d - 1), piece))
            if d > 1:
                pl.when(z + d - 1 < layers)(lambda: from_across(z + d - 1, piece))

    for layer in range(layers):
        for row in range(2):
            for piece in range(PIECES):
                copy(3, slot_of(layer, row, 1 - core), piece, sibling).wait_recv()
    own.wait()
    for layer in range(layers):
        slot = slot_of(layer, y, core)
        for piece in range(PIECES):
            pl.when(jnp.logical_and(has_above, layer <= z))(lambda: copy(0, slot, piece, above).wait_send())
            pl.when(jnp.logical_and(has_below, layer >= z))(lambda: copy(1, slot, piece, below).wait_send())
            copy(2, slot, piece, across).wait_send()
            copy(3, slot, piece, sibling).wait_send()
            copy(3, slot_of(layer, 1 - y, core), piece, sibling).wait_send()


def gather(samples, devices):
    if devices != 16:
        return lax.all_gather(samples, "tm", axis=0, tiled=True)
    return pl.pallas_call(
        functools.partial(gather_kernel, devices // 4),
        in_specs=[pl.BlockSpec(memory_space=pl.ANY)],
        out_specs=pl.BlockSpec(memory_space=pl.ANY),
        out_shape=jax.ShapeDtypeStruct((devices * samples.shape[0], samples.shape[1]), samples.dtype),
        scratch_shapes=[
            pltpu.SemaphoreType.DMA,
            pltpu.SemaphoreType.DMA((4, devices, PIECES)),
            pltpu.SemaphoreType.DMA((devices, PIECES)),
        ],
        compiler_params=pltpu.CompilerParams(collective_id=0, has_side_effects=True),
    )(samples)


def whiten_kernel(seg_count, per_step, x_ref, f_ref, band_ref, w_ref, amp_ref, spec, column, inv_amp):
    step = pl.program_id(1)
    rounds = seg_count // per_step
    chans = x_ref.shape[1]

    @pl.when(step < rounds)
    def _():
        rows = jnp.concatenate([x_ref[s * SEG : (s + 1) * SEG, :].T for s in range(per_step)], axis=0)
        q = HBIN
        scale = 1.0 / math.sqrt(SEG)
        for at in range(0, NBIN, q):
            re = jnp.dot(rows, f_ref[:, at : at + q], preferred_element_type=jnp.float32) * scale
            im = jnp.dot(rows, f_ref[:, NBIN + at : NBIN + at + q], preferred_element_type=jnp.float32) * scale
            magnitude = jnp.sqrt(re * re + im * im)
            col = jnp.zeros((chans, q), jnp.float32)
            for s in range(per_step):
                piece = slice(s * chans, (s + 1) * chans)
                spec[step * per_step + s, 0, :, at : at + q] = re[piece]
                spec[step * per_step + s, 1, :, at : at + q] = im[piece]
                col = col + magnitude[piece]

            @pl.when(step == 0)
            def _():
                column[:, at : at + q] = col

            @pl.when(step > 0)
            def _():
                column[:, at : at + q] += col

    @pl.when(step == rounds)
    def _():
        col = column[...]
        high = col.astype(jnp.bfloat16)
        low = (col - high.astype(jnp.float32)).astype(jnp.bfloat16)
        both = jnp.dot(
            jnp.concatenate([high, low], axis=0), band_ref[...], preferred_element_type=jnp.float32
        )
        window = both[:chans] + both[chans:]
        amp = window * (1.0 / float((2 * SMOOTH + 1) * seg_count)) + 1e-06
        amp_ref[...] = amp
        inv_amp[...] = 1.0 / amp

    @pl.when(step >= rounds)
    def _():
        for s in range(per_step):
            for c in range(2):
                w_ref[2 * s + c] = (spec[(step - rounds) * per_step + s, c] * inv_amp[...]).astype(jnp.bfloat16)


def whiten(samples, seg_count):
    per_step = min(seg_count, 4)
    rounds = seg_count // per_step
    channels = samples.shape[1]
    chans = CHANS if rounds == 1 else BLK
    return pl.pallas_call(
        functools.partial(whiten_kernel, seg_count, per_step),
        grid=(channels // chans, 2 * rounds),
        in_specs=[
            pl.BlockSpec((per_step * SEG, chans), lambda h, s: (jnp.minimum(s, rounds - 1), h)),
            pl.BlockSpec((SEG, 2 * NBIN), lambda h, s: (0, 0), pipeline_mode=pl.Buffered(1)),
            pl.BlockSpec((NBIN, NBIN), lambda h, s: (0, 0)),
        ],
        out_specs=[
            pl.BlockSpec((2 * per_step, chans, NBIN), lambda h, s: (jnp.maximum(s - rounds, 0), h, 0)),
            pl.BlockSpec((chans, NBIN), lambda h, s: (h, 0)),
        ],
        out_shape=[
            jax.ShapeDtypeStruct((2 * seg_count, channels, NBIN), jnp.bfloat16),
            jax.ShapeDtypeStruct((channels, NBIN), jnp.float32),
        ],
        scratch_shapes=[
            pltpu.VMEM((seg_count, 2, chans, NBIN), jnp.float32),
            pltpu.VMEM((chans, NBIN), jnp.float32),
            pltpu.VMEM((chans, NBIN), jnp.float32),
        ],
        compiler_params=pltpu.CompilerParams(vmem_limit_bytes=60 * MIB),
    )(samples, jnp.asarray(forward_constant()), jnp.asarray(band_constant()))


def cross_terms(u_ref, v_ref, row, segs, base, k0):
    re = im = None
    for s in range(segs):
        at = base + 2 * s
        u0 = u_ref[at, pl.ds(row, 1), k0 : k0 + KCH]
        u1 = u_ref[at + 1, pl.ds(row, 1), k0 : k0 + KCH]
        u0 = jnp.broadcast_to(u0, (16, KCH)).astype(jnp.bfloat16)[None]
        u1 = jnp.broadcast_to(u1, (16, KCH)).astype(jnp.bfloat16)[None]
        v0 = v_ref[at, :, k0 : k0 + KCH].reshape(BLK // 16, 16, KCH)
        v1 = v_ref[at + 1, :, k0 : k0 + KCH].reshape(BLK // 16, 16, KCH)
        r = u0 * v0 + u1 * v1
        i = u1 * v0 - u0 * v1
        re = r if re is None else re + r
        im = i if im is None else im + i
    return re.reshape(BLK, KCH), im.reshape(BLK, KCH)


def lags_kernel(seg_count, together, unit, lefts_ref, blocks_ref, left_ref, v_ref, inv_ref, out_ref, u_ref):
    scale = 1.0 / (seg_count * math.sqrt(NBIN))
    u_ref[...] = left_ref[...].astype(jnp.float32)

    def body(g, carry):
        acc = jnp.zeros((together * BLK, LAGS), jnp.float32)
        for k0 in range(0, NBIN, KCH):
            res, ims = [], []
            for q in range(together):
                row = g * together + q
                if seg_count <= 4:
                    re, im = cross_terms(u_ref, v_ref, row, seg_count, 0, k0)
                else:

                    def more(j, held):
                        re, im = cross_terms(u_ref, v_ref, row, 4, j * 8, k0)
                        return held[0] + re.astype(jnp.float32), held[1] + im.astype(jnp.float32)

                    zero = jnp.zeros((BLK, KCH), jnp.float32)
                    re, im = lax.fori_loop(0, seg_count // 4, more, (zero, zero))
                    re, im = re.astype(jnp.bfloat16), im.astype(jnp.bfloat16)
                res.append(re)
                ims.append(im)
            acc = acc + jnp.dot(
                jnp.concatenate(res, axis=0), inv_ref[0, k0 : k0 + KCH, :], preferred_element_type=jnp.float32
            )
            acc = acc + jnp.dot(
                jnp.concatenate(ims, axis=0), inv_ref[1, k0 : k0 + KCH, :], preferred_element_type=jnp.float32
            )
        for q in range(together):
            out_ref[g * together + q] = acc[q * BLK : (q + 1) * BLK] * scale
        return carry

    if unit == together:
        body(0, 0)
    else:
        lax.fori_loop(0, unit // together, body, 0)


def lags(whitened, left_rows, left_units, right_blocks, seg_count, unit):
    groups = right_blocks.shape[0]
    together = math.gcd(unit, 8)
    if left_rows is None:
        left_rows = whitened
        left_spec = pl.BlockSpec((2 * seg_count, unit, NBIN), lambda g, lefts, blocks: (0, lefts[g], 0))
    else:
        left_spec = pl.BlockSpec((None, 2 * seg_count, unit, NBIN), lambda g, lefts, blocks: (g, 0, 0, 0))
    return pl.pallas_call(
        functools.partial(lags_kernel, seg_count, together, unit),
        grid_spec=pltpu.PrefetchScalarGridSpec(
            num_scalar_prefetch=2,
            grid=(groups,),
            in_specs=[
                left_spec,
                pl.BlockSpec((2 * seg_count, BLK, NBIN), lambda g, lefts, blocks: (0, blocks[g], 0)),
                pl.BlockSpec((2, NBIN, LAGS), lambda g, lefts, blocks: (0, 0, 0)),
            ],
            out_specs=pl.BlockSpec((unit, BLK, LAGS), lambda g, lefts, blocks: (g, 0, 0)),
            scratch_shapes=[pltpu.VMEM((2 * seg_count, unit, NBIN), jnp.float32)],
        ),
        out_shape=jax.ShapeDtypeStruct((groups * unit, BLK, LAGS), jnp.float32),
        compiler_params=pltpu.CompilerParams(vmem_limit_bytes=60 * MIB),
    )(left_units, right_blocks, left_rows, whitened, jnp.asarray(inverse_constant()))


def per_device(samples, block_pairs):
    devices = lax.axis_size("tm")
    position = lax.axis_index("tm")
    shard_len, channels = samples.shape
    seg_count = devices * shard_len // SEG
    bin_count = NBIN // devices
    rows = block_pairs.shape[0] * BLK // devices
    gathered = gather(samples, devices)
    whitened, amp = whiten(gathered, seg_count)

    unit = math.gcd(rows, BLK)
    starts = position * rows + unit * jnp.arange(rows // unit, dtype=jnp.int32)
    pair = starts // BLK
    left_starts = block_pairs[pair, 0] * BLK + starts % BLK
    right_blocks = block_pairs[pair, 1]
    left_rows = None
    if unit % 16:
        left_rows = jnp.stack(
            [
                lax.dynamic_slice_in_dim(whitened, left_starts[g], unit, axis=1)
                for g in range(rows // unit)
            ]
        )
    lag_values = lags(whitened, left_rows, left_starts // unit, right_blocks, seg_count, unit)

    amplitude = lax.dynamic_slice_in_dim(amp, position * bin_count, bin_count, axis=1).T
    return (lag_values, amplitude)


def solution(mesh):
    placed = (P(("win", "tm"), None), P())
    return jax.shard_map(
        per_device,
        mesh=mesh,
        in_specs=placed,
        out_specs=(P(("win", "tm"), None, None), P(("win", "tm"), None)),
        check_vma=False,
    )
```
